128 devices in a mesh: pair: 4 (over z), virt: 32 (over y, x, core).
Axes of the slice: x: 4, y: 4, z: 4, core: 2. Of those that a mesh axis runs over, the one named last changes fastest.
Arguments:
- amps: bfloat16 [2048, 24576], P('pair', 'virt'), may hold values from -6 to 6
- ints: bfloat16 [24576, 24576], P('pair', 'virt'), may hold values from -0.0390625 to 0.0390625
- amp_mask: int32 [16, 192], P('pair', 'virt'), may hold values 0 or 1
- int_mask: int32 [192, 192], P('pair', 'virt'), may hold values 0 or 1
- vir_energy: float32 [24576], P('virt'), may hold values from 0.5 to 3
- pair_energy: float32 [2048], P('pair'), may hold values from -2 to -0.5
Outputs:
- updated: float32 [2048, 24576], P('pair', 'virt')
The draws below stay inside these ranges and needn't reach their ends.
All inputs are finite; a program needn't handle non-finite values. No bound on the sum of `amp_mask` or of `int_mask` on one device may be relied on, other than what follows from the above.
Results may differ from the reference program's by a relative error of at most 0.0003.
Values may be sent and summed in bfloat16 or wider, within the bound.
No kernel may reach another device: no remote copies, remote signals or barrier semaphores. Data moves between devices by JAX's collectives and lax.ppermute only.
A program may use at most 192 MiB of HBM per device.

```python
import jax
import jax.numpy as jnp

NV = 24576
TILE = 128
ROWS = 2048


def place_ends(result, rng, low, largest):
    extent = result.shape
    index_at = [jax.random.randint(jax.random.fold_in(rng, axis), (), 0, extent[axis]) for axis in range(len(extent))]
    result = result.at[tuple(index_at)].set(low)
    longest = extent.index(max(extent))
    index_at[longest] = (index_at[longest] + 1) % extent[longest]
    return result.at[tuple(index_at)].set(largest)


def block_levels(key, extent, pieces, least, top_value):
    gain = 1.0
    for dim, parts in pieces:
        heights = jax.random.uniform(jax.random.fold_in(jax.random.fold_in(key, 6), dim), (parts,), jnp.float32, least / len(pieces), top_value / len(pieces))
        gain = gain * jnp.repeat(jnp.exp(heights), extent[dim] // parts).reshape((-1,) + (1,) * (len(extent) - 1 - dim))
    return gain


def scatter_about(rng, dims, deviation, bound, pieces=(), kind=jnp.bfloat16):
    values = jax.random.normal(rng, dims, jnp.float32) * deviation
    if len(pieces) > 0:
        values = block_levels(rng, dims, pieces, -0.22, 0.18) * values
    return jnp.clip(values, min=-bound, max=bound).astype(kind)


def setup_inputs(seed: int = 0) -> dict:
    splits = jax.random.split(jax.random.key(seed), 7)
    amps = scatter_about(splits[0], (ROWS, NV), 1.0, 6.0, ((0, 4), (1, 32)))
    ints = scatter_about(splits[1], (NV, NV), NV ** -0.5, 0.0390625, ((0, 4), (1, 32)))
    amp_mask = place_ends((jax.random.randint(splits[2], (ROWS // TILE, NV // TILE), 0, 2) < 1).astype(jnp.int32), jax.random.fold_in(splits[2], 1), 0, 1)
    int_mask = place_ends((jax.random.randint(splits[3], (NV // TILE, NV // TILE), 0, 2) < 1).astype(jnp.int32), jax.random.fold_in(splits[3], 1), 0, 1)
    vir_energy = jnp.clip(0.5 + 2.5 * jax.random.uniform(splits[4], (NV,), jnp.float32) ** block_levels(splits[4], (NV,), ((0, 32),), -0.2, 0.2), 0.5, 3.0)
    pair_energy = jnp.clip(-2.0 + 1.5 * jax.random.uniform(splits[5], (ROWS,), jnp.float32) ** block_levels(splits[5], (ROWS,), ((0, 4),), -0.2, 0.2), -2.0, -0.5)
    return {"amps": amps, "ints": ints, "amp_mask": amp_mask, "int_mask": int_mask, "vir_energy": vir_energy, "pair_energy": pair_energy}


def widen(mask):
    return jnp.repeat(jnp.repeat(mask.astype(jnp.bfloat16), TILE, 0), TILE, 1)


def reference(amps, ints, amp_mask, int_mask, vir_energy, pair_energy):
    screened = amps * widen(amp_mask)
    kept = ints * widen(int_mask)
    contracted = jnp.dot(screened, kept, preferred_element_type=jnp.float32)
    denom = vir_energy[None, :] - pair_energy[:, None]
    return amps.astype(jnp.float32) + contracted / denom
```

```python
import functools

import jax
import jax.numpy as jnp
import numpy as np
from jax import lax
from jax.experimental import pallas as pl
from jax.experimental.pallas import tpu as pltpu
from jax.sharding import PartitionSpec as P

TILE = 128
AXES = ("pair", "virt")
N = 4
SENT = jnp.float16
FLIP = {0: 0, 1: -1, -1: 1, 2: 2}


def lin(z, y, x, c):
    return ((z % N) * N + y % N) * 2 * N + (x % N) * 2 + c


def permute(arr, to):
    pairs = [
        (lin(z, y, x, c), lin(*to(z, y, x, c)))
        for z in range(N)
        for y in range(N)
        for x in range(N)
        for c in range(2)
    ]
    return lax.ppermute(arr, AXES, pairs)


def side(c):
    return -1 if c == 0 else 1


def swap(arr):
    return permute(arr, lambda z, y, x, c: (z, y, x, 1 - c))


def shift(arr, axis):
    if axis == "x":
        return permute(arr, lambda z, y, x, c: (z, y, x - side(c), c))
    return permute(arr, lambda z, y, x, c: (z, y - side(c), x, c))


def swapped(item):
    arr, labels = item
    return swap(arr), [(FLIP[f], FLIP[s], 1 - k) for f, s, k in labels]


def along(item, axis, place):
    arr, labels = item
    moved = []
    for lab in labels:
        lab = list(lab)
        lab[place] = {0: 1, 1: 2}[lab[place]]
        moved.append(tuple(lab))
    return shift(arr, axis), moved


def take(item, lo, hi):
    return item[0][lo:hi], item[1][lo:hi]


def gather(own, first, second, early, late):
    own = (own, [(0, 0, 0)])
    other = swapped(own)
    both = (jnp.concatenate([own[0], other[0]], 0), own[1] + other[1])
    near = along(both, first, 0)
    far_side = swapped(near)
    far = along(take(near, 0, 1), first, 0)
    far_other = swapped(far)
    blocks = {}
    for arr, labels in (own, other, near, far_side, far, far_other):
        for i, lab in enumerate(labels):
            blocks[lab] = arr[i : i + 1]
    items = []
    for offs in (early, late):
        labels = [(f, 0, k) for k in (0, 1) for f in offs]
        group = (jnp.concatenate([blocks[lab] for lab in labels], 0), labels)
        near2 = along(group, second, 1)
        far2 = along(take(near2, 0, len(offs)), second, 1)
        items += [group, near2, swapped(near2), far2, swapped(far2)]
    return items


def screen_amps(mask_ref, amps_ref, a_ref, b_ref):
    rows = a_ref.shape[1]
    for i in range(amps_ref.shape[0] // TILE):
        out, r = (a_ref, i * TILE) if i * TILE < rows else (b_ref, i * TILE - rows)
        for j in range(amps_ref.shape[1] // TILE):
            tile = amps_ref[i * TILE : (i + 1) * TILE, j * TILE : (j + 1) * TILE]
            out[0, r : r + TILE, j * TILE : (j + 1) * TILE] = jnp.where(mask_ref[i, j] != 0, tile, jnp.zeros_like(tile))


def screen_ints(mask_ref, ints_ref, out_ref):
    step = pl.program_id(0)
    n = ints_ref.shape[1] // TILE
    for i in range(n):
        for j in range(ints_ref.shape[2] // TILE):
            tile = ints_ref[0, i * TILE : (i + 1) * TILE, j * TILE : (j + 1) * TILE]
            out_ref[0, i * TILE : (i + 1) * TILE, j * TILE : (j + 1) * TILE] = jnp.where(
                mask_ref[step * n + i, j] != 0, tile, jnp.zeros_like(tile)
            )


def product_kernel(bounds, table_ref, where_ref, *refs):
    *a_refs, kept_ref, out_ref, acc_ref = refs
    s = pl.program_id(0)
    for (lo, hi), a_ref in zip(bounds, a_refs):

        @pl.when((s >= lo) & (s < hi))
        def _():
            part = jnp.dot(a_ref[0], kept_ref[0], preferred_element_type=jnp.float32)
            if lo == 0:

                @pl.when(s == 0)
                def _():
                    acc_ref[...] = part

                @pl.when(s != 0)
                def _():
                    acc_ref[...] += part
            else:
                acc_ref[...] += part

    @pl.when(s == bounds[-1][1] - 1)
    def _():
        out_ref[...] = acc_ref[...].astype(out_ref.dtype)


def product(chosen, kept, where):
    bounds, total = [], 0
    for _, positions, _ in chosen:
        bounds.append((total, total + len(positions)))
        total += len(positions)
    table = np.zeros((len(chosen) + 1, total), np.int32)
    for i, ((_, positions, ks), (lo, hi)) in enumerate(zip(chosen, bounds)):
        table[i, :lo], table[i, lo:hi], table[i, hi:] = positions[0], positions, positions[-1]
        table[-1, lo:hi] = ks
    rows, depth = chosen[0][0].shape[1:]
    width = kept.shape[2]
    a_specs = [pl.BlockSpec((1, rows, depth), lambda s, t, w, i=i: (t[i, s], 0, 0)) for i in range(len(chosen))]
    return pl.pallas_call(
        functools.partial(product_kernel, bounds),
        grid_spec=pltpu.PrefetchScalarGridSpec(
            num_scalar_prefetch=2,
            grid=(total,),
            in_specs=a_specs + [pl.BlockSpec((1, depth, width), lambda s, t, w: (w[t[len(chosen), s]], 0, 0))],
            out_specs=pl.BlockSpec((rows, width), lambda s, t, w: (0, 0)),
            scratch_shapes=[pltpu.VMEM((rows, width), jnp.float32)],
        ),
        out_shape=jax.ShapeDtypeStruct((rows, width), jnp.float32),
        compiler_params=pltpu.CompilerParams(vmem_limit_bytes=24 << 20),
        cost_estimate=pl.CostEstimate(
            flops=2 * rows * depth * width * total,
            bytes_accessed=2 * total * depth * (rows + width) + 4 * rows * width,
            transcendentals=0,
        ),
    )(jnp.asarray(table), where, *[c[0] for c in chosen], kept)


K_INDEX = {(off, k): i for i, (off, k) in enumerate((o, k) for o in (0, 1, -1, 2) for k in (0, 1))}


def pieces(items, row_place, kept, where):
    got = []
    for off in (0, 1, -1, 2):
        chosen = []
        for arr, labels in items:
            hits = [i for i, lab in enumerate(labels) if lab[row_place] == off]
            if hits:
                chosen.append((arr, hits, [K_INDEX[labels[i][1 - row_place], labels[i][2]] for i in hits]))
        part = product(chosen, kept, where).astype(SENT)
        got.append(permute(part, lambda z, y, x, c, off=off: (z + y + off * (side(c) if abs(off) == 1 else 1), y, x, c)))
    return got


def on_device(amps, ints, amp_mask, int_mask, vir_energy, pair_energy):
    rows, depth = amps.shape
    half = rows // 2
    part = jax.ShapeDtypeStruct((1, half, depth), amps.dtype)
    upper, lower = pl.pallas_call(
        screen_amps,
        in_specs=[pl.BlockSpec(memory_space=pltpu.SMEM), pl.BlockSpec(memory_space=pltpu.VMEM)],
        out_specs=[pl.BlockSpec(memory_space=pltpu.VMEM)] * 2,
        out_shape=[part, part],
    )(amp_mask, amps)
    to_plane = lambda z, y, x, c: (y, z - y, x, c)
    upper, lower = permute(upper, to_plane), permute(lower, to_plane)
    blocks = ints.shape[0] // depth
    kept = pl.pallas_call(
        screen_ints,
        grid_spec=pltpu.PrefetchScalarGridSpec(
            num_scalar_prefetch=1,
            grid=(blocks,),
            in_specs=[pl.BlockSpec((1, depth, ints.shape[1]), lambda s, m: (s, 0, 0))],
            out_specs=pl.BlockSpec((1, depth, ints.shape[1]), lambda s, m: (s, 0, 0)),
        ),
        out_shape=jax.ShapeDtypeStruct((blocks, depth, ints.shape[1]), ints.dtype),
    )(int_mask, ints.reshape(blocks, depth, ints.shape[1]))
    virt = lax.axis_index("virt")
    core, x = virt % 2, (virt // 2) % N
    d = 2 * core - 1
    where = jnp.stack([((x + off * (d if abs(off) == 1 else 1)) % N) * 2 + (core if k == 0 else 1 - core) for off, k in K_INDEX])
    got_upper = pieces(gather(upper, "x", "y", (0, 1, -1), (2,)), 1, kept, where)
    got_lower = pieces(gather(lower, "y", "x", (1, -1, 2), (0,)), 0, kept, where)
    total = lambda got: sum(g.astype(jnp.float32) for g in got)
    contracted = jnp.concatenate([total(got_upper), total(got_lower)], 0)
    denom = vir_energy[None, :] - pair_energy[:, None]
    return amps.astype(jnp.float32) + contracted / denom


def solution(mesh):
    return jax.shard_map(
        on_device,
        mesh=mesh,
        in_specs=(
            P("pair", "virt"),
            P("pair", "virt"),
            P("pair", "virt"),
            P("pair", "virt"),
            P("virt"),
            P("pair"),
        ),
        out_specs=P("pair", "virt"),
        check_vma=False,
    )
```

```python
import functools

import jax
import jax.numpy as jnp
import numpy as np
from jax import lax
from jax.experimental import pallas as pl
from jax.experimental.pallas import tpu as pltpu
from jax.sharding import PartitionSpec as P

TILE = 128
AXES = ("pair", "virt")
N = 4
SENT = jnp.float16
FLIP = {0: 0, 1: -1, -1: 1, 2: 2}


def lin(z, y, x, c):
    return ((z % N) * N + y % N) * 2 * N + (x % N) * 2 + c


def permute(arr, to):
    pairs = [
        (lin(z, y, x, c), lin(*to(z, y, x, c)))
        for z in range(N)
        for y in range(N)
        for x in range(N)
        for c in range(2)
    ]
    return lax.ppermute(arr, AXES, pairs)


def side(c):
    return -1 if c == 0 else 1


def swap(arr):
    return permute(arr, lambda z, y, x, c: (z, y, x, 1 - c))


def shift(arr, axis):
    if axis == "x":
        return permute(arr, lambda z, y, x, c: (z, y, x - side(c), c))
    return permute(arr, lambda z, y, x, c: (z, y - side(c), x, c))


def swapped(item):
    (arr,), offs, koffs, flip = item
    return (swap(arr),), tuple(FLIP[o] for o in offs), tuple(FLIP[o] for o in koffs), not flip


def tie(value, *others):
    return lax.optimization_barrier((value, *others))[0]


def first_round(own, other, axis):
    near = shift(jnp.concatenate([own, other], 0), axis)
    far = shift(near[:1], axis)
    near_swapped, far_swapped = swap(near), swap(far)
    return {
        (0, 0): own,
        (0, 1): other,
        (1, 0): near[:1],
        (1, 1): near[1:],
        (-1, 1): near_swapped[:1],
        (-1, 0): near_swapped[1:],
        (2, 0): far,
        (2, 1): far_swapped,
    }


def screen_amps(mask_ref, amps_ref, *out_refs):
    starts = np.cumsum([0] + [o.shape[1] for o in out_refs]).tolist()
    for out_ref, lo, hi in zip(out_refs, starts, starts[1:]):
        for top in range(lo, hi, TILE):
            top_tile = top // TILE
            end = min(hi, (top_tile + 1) * TILE)
            for j in range(amps_ref.shape[1] // TILE):
                tile = amps_ref[top:end, j * TILE : (j + 1) * TILE]
                out_ref[0, top - lo : end - lo, j * TILE : (j + 1) * TILE] = jnp.where(
                    mask_ref[top_tile, j] != 0, tile, jnp.zeros_like(tile)
                )


def screen_ints(mask_ref, ints_ref, out_ref):
    step = pl.program_id(0)
    n = ints_ref.shape[0] // TILE
    for i in range(n):
        for j in range(ints_ref.shape[1] // TILE):
            tile = ints_ref[i * TILE : (i + 1) * TILE, j * TILE : (j + 1) * TILE]
            out_ref[i * TILE : (i + 1) * TILE, j * TILE : (j + 1) * TILE] = jnp.where(
                mask_ref[step * n + i, j] != 0, tile, jnp.zeros_like(tile)
            )


OFFS = (0, 1, -1, 2)
CORE = 4


def product_kernel(phases, n_init, n_out, table_ref, where_ref, *refs):
    n = sum(count for _, _, lanes in phases for count, _, _ in lanes)
    a_refs, kept_ref, init_refs, out_refs = refs[:n], refs[n], refs[n + 1 : n + 1 + n_init], refs[-n_out:]
    s = pl.program_id(0)
    core = where_ref[CORE]
    rows = out_refs[0].shape[0]

    def add(places, lanes):
        sides = []
        for first, second in lanes:
            sides.append(jnp.concatenate([first, second], -1))
        a = sides[0] if len(sides) == 1 else jnp.concatenate(sides, 0)
        part = jnp.dot(a, kept_ref[...], preferred_element_type=jnp.float32)
        for i, o in enumerate(places):
            mine = part[i * rows : (i + 1) * rows]

            @pl.when(s == 0)
            def _():
                out_refs[o][...] = mine + init_refs[o][...] if n_init else mine

            @pl.when(s != 0)
            def _():
                out_refs[o][...] += mine

    at = 0
    for lo, hi, lanes in phases:
        places, blocks, split = [], [], None
        for count, order, flip in lanes:
            places += order
            if count == 2:
                split = a_refs[at], a_refs[at + 1]
            elif flip is None:
                blocks.append((a_refs[at], 0))
            else:
                blocks.append((a_refs[at], 1 - core if flip else core))
            at += count

        if split is None:

            @pl.when((s >= lo) & (s < hi))
            def _():
                add(places, [(ref[0, i], ref[0, 1 - i]) for ref, i in blocks])
        else:
            for here in (0, 1):

                @pl.when((s >= lo) & (s < hi) & (core == here))
                def _():
                    other = split[1][0]
                    if len(places) > 1:
                        turned = [places.index(OFFS.index(FLIP[OFFS[o]])) for o in places]
                        other = jnp.concatenate([other[i * rows : (i + 1) * rows] for i in turned], 0)
                    pair = split[0][0], other
                    add(places, [pair if here == 0 else pair[::-1]])


def product(groups, offs, kept, where, init=()):
    phases, total = [], 0
    for group in groups:
        steps = len(group[0][2])
        phases.append((total, total + steps, [(len(arrs), [offs.index(o) for o in order], flip) for arrs, order, _, flip in group]))
        total += steps
    arrs, table = [], []
    where_row = np.zeros(total, np.int32)
    for group, (lo, hi, _) in zip(groups, phases):
        wanted = group[0][2]
        for item in group:
            for i, arr in enumerate(item[0]):
                stored = item[2] if i == 0 else tuple(FLIP[o] for o in item[2])
                places = [stored.index(o) for o in wanted]
                row = np.zeros(total, np.int32)
                row[:lo], row[lo:hi], row[hi:] = places[0], places, places[-1]
                arrs.append(arr)
                table.append(row)
        where_row[lo:hi] = [OFFS.index(o) for o in wanted]
    table = np.stack(table + [where_row])
    rows, depth = arrs[0].shape[-2] // len(groups[0][0][1]), arrs[0].shape[-1]
    width, nf = kept.shape[1], len(offs)
    a_specs = [
        pl.BlockSpec((1,) + arr.shape[1:], lambda s, t, w, i=i, nd=arr.ndim: (t[i, s],) + (0,) * (nd - 1))
        for i, arr in enumerate(arrs)
    ]
    flat = pl.BlockSpec((rows, width), lambda s, t, w: (0, 0))
    return pl.pallas_call(
        functools.partial(product_kernel, phases, len(init), nf),
        grid_spec=pltpu.PrefetchScalarGridSpec(
            num_scalar_prefetch=2,
            grid=(total,),
            in_specs=a_specs
            + [pl.BlockSpec((2 * depth, width), lambda s, t, w: (w[t[len(arrs), s]], 0))]
            + [flat] * len(init),
            out_specs=[flat] * nf,
        ),
        out_shape=[jax.ShapeDtypeStruct((rows, width), jnp.float32)] * nf,
        compiler_params=pltpu.CompilerParams(vmem_limit_bytes=VMEM_BYTES),
        cost_estimate=pl.CostEstimate(
            flops=rows * nf * depth * width * total // 4,
            bytes_accessed=total * depth * (nf * rows + width) // 4,
            transcendentals=0,
        ),
    )(jnp.asarray(table), where, *arrs, kept, *init)


VMEM_BYTES = 16 << 20


M_ROWS = 256


def product_plane_kernel(ys, planes_ref, kept_ref, *refs):
    out_refs, (a_buf, b_buf, a_sem, b_sem) = refs[: len(ys)], refs[len(ys) :]
    rows, depth = a_buf.shape[-2:]

    def copies(step):
        kept = pltpu.make_async_copy(kept_ref.at[pl.ds(step * 2 * depth, 2 * depth)], b_buf.at[step], b_sem.at[step])
        return [kept] + [
            pltpu.make_async_copy(planes_ref.at[y, pl.ds(2 * step, 2)], a_buf.at[step, i], a_sem.at[step, i])
            for i, y in enumerate(ys)
        ]

    for step in range(N):
        for copy in copies(step):
            copy.start()
    for step in range(N):
        for copy in copies(step):
            copy.wait()
        for i, out_ref in enumerate(out_refs):
            for m in range(0, rows, M_ROWS):
                here = slice(m, min(m + M_ROWS, rows))
                a = jnp.concatenate([a_buf[step, i, 0, here], a_buf[step, i, 1, here]], -1)
                part = jnp.dot(a, b_buf[step], preferred_element_type=jnp.float32)
                out_ref[here] = part if step == 0 else out_ref[here] + part


def product_plane(planes, ys, kept):
    _, _, rows, depth = planes.shape
    width = kept.shape[1]
    return pl.pallas_call(
        functools.partial(product_plane_kernel, ys),
        in_specs=[pl.BlockSpec(memory_space=pltpu.HBM)] * 2,
        out_specs=[pl.BlockSpec(memory_space=pltpu.VMEM)] * len(ys),
        out_shape=[jax.ShapeDtypeStruct((rows, width), jnp.float32)] * len(ys),
        scratch_shapes=[
            pltpu.VMEM((N, len(ys), 2, rows, depth), planes.dtype),
            pltpu.VMEM((N, 2 * depth, width), kept.dtype),
            pltpu.SemaphoreType.DMA((N, len(ys))),
            pltpu.SemaphoreType.DMA((N,)),
        ],
        compiler_params=pltpu.CompilerParams(vmem_limit_bytes=30 << 20),
        cost_estimate=pl.CostEstimate(
            flops=4 * N * len(ys) * rows * depth * width,
            bytes_accessed=4 * N * depth * (len(ys) * rows + width) + 4 * len(ys) * rows * width,
            transcendentals=0,
        ),
    )(planes, kept)


def to_owner(part, off):
    step = lambda c: off * side(c) if abs(off) == 1 else off
    return permute(part.astype(SENT), lambda z, y, x, c: (z + y + step(c), y, x, c))


S_ROWS, A_ROWS, B_ROWS = 384, 64, 64


def on_device(amps, ints, amp_mask, int_mask, vir_energy, pair_energy):
    rows, depth = amps.shape
    split = (S_ROWS, A_ROWS, B_ROWS)
    screened = pl.pallas_call(
        screen_amps,
        in_specs=[pl.BlockSpec(memory_space=pltpu.SMEM), pl.BlockSpec(memory_space=pltpu.VMEM)],
        out_specs=[pl.BlockSpec(memory_space=pltpu.VMEM)] * len(split),
        out_shape=[jax.ShapeDtypeStruct((1, r, depth), amps.dtype) for r in split],
    )(amp_mask, amps)
    s_part, a_part, b_part = [permute(part, lambda z, y, x, c: (y, z - y, x, c)) for part in screened]
    width = ints.shape[1]
    kept = pl.pallas_call(
        screen_ints,
        grid_spec=pltpu.PrefetchScalarGridSpec(
            num_scalar_prefetch=1,
            grid=(ints.shape[0] // depth,),
            in_specs=[pl.BlockSpec((depth, width), lambda s, m: (s, 0))],
            out_specs=pl.BlockSpec((depth, width), lambda s, m: (s, 0)),
        ),
        out_shape=jax.ShapeDtypeStruct(ints.shape, ints.dtype),
        compiler_params=pltpu.CompilerParams(vmem_limit_bytes=VMEM_BYTES),
    )(int_mask, ints)
    virt = lax.axis_index("virt")
    core, x = virt % 2, (virt // 2) % N
    d = 2 * core - 1
    where = jnp.stack([(x + o * (d if abs(o) == 1 else 1)) % N for o in OFFS] + [core]).astype(jnp.int32)

    a_pair, b_pair = swap(a_part), swap(b_part)
    s_part, a_pair, b_pair = lax.optimization_barrier((s_part, a_pair, b_pair))
    planes = lax.all_gather(s_part[0], "virt", axis=0).reshape(N, 2 * N, S_ROWS, depth)
    round_a, round_b = first_round(a_part, a_pair, "x"), first_round(b_part, b_pair, "y")
    a_own = ((jnp.concatenate([round_a[o, k] for o in OFFS for k in (0, 1)], 0).reshape(N, 2, A_ROWS, depth),), (0,), OFFS, False)
    b_own = (
        (jnp.concatenate([round_b[o, k] for k in (0, 1) for o in OFFS], 0).reshape(1, 2, N * B_ROWS, depth),),
        OFFS,
        (0,),
        False,
    )
    a_near, b_near = ((shift(a_own[0][0], "y"),), (1,), OFFS, False), ((shift(b_own[0][0], "x"),), OFFS, (1,), False)
    a_next, b_next = a_near[0][0][:, 0], b_near[0][0][:, 0]
    a_next, b_next, kept = lax.optimization_barrier((a_next, b_next, kept))
    a_far, b_far = shift(a_next, "y"), shift(b_next, "x")
    a_side, b_side = swapped(a_near), swapped(b_near)

    b_early = product([[b_own], [b_near], [b_side]], OFFS, kept, where)
    a_early = product([[a_own, a_near, a_side]], OFFS[:3], kept, where)
    a_far, b_far = lax.optimization_barrier((a_far, b_far, b_early, a_early))[:2]
    a_other, b_other = swap(a_far), swap(b_far)
    b_done = product([[((b_far, b_other), OFFS, (2,), False)]], OFFS, kept, where, b_early)
    a_last = product([[((a_far, a_other), (2,), OFFS, False)]], (2,), kept, where)
    p_got = [
        to_owner(jnp.concatenate([a, b], 0), o) for a, b, o in zip([*a_early, *a_last], b_done, OFFS)
    ]
    planes, *p_got = lax.optimization_barrier((planes, *p_got))
    turn = lambda part, i: permute(part.astype(SENT), lambda z, y, x, c: (z + i, y, x, c))
    mid = S_ROWS // 2
    (across,) = product_plane(planes, (2,), kept)
    low, high = turn(across[:mid], 1), turn(across[mid:], 3)
    up, down = product_plane(planes, (1, 3), kept)
    up = jnp.concatenate([up[:mid] + low.astype(jnp.float32), up[mid:]], 0).astype(SENT)
    down = jnp.concatenate([down[:mid], down[mid:] + high.astype(jnp.float32)], 0).astype(SENT)
    planes, up, down = lax.optimization_barrier((planes, up, down))
    up, down = turn(up, 1), turn(down, 3)
    (here,) = product_plane(planes, (0,), kept)
    s_got = [here, up, down]

    total = lambda got: sum(g.astype(jnp.float32) for g in got)
    contracted = jnp.concatenate([total(s_got), total(p_got)], 0)
    denom = vir_energy[None, :] - pair_energy[:, None]
    return amps.astype(jnp.float32) + contracted / denom


def solution(mesh):
    return jax.shard_map(
        on_device,
        mesh=mesh,
        in_specs=(
            P("pair", "virt"),
            P("pair", "virt"),
            P("pair", "virt"),
            P("pair", "virt"),
            P("virt"),
            P("pair"),
        ),
        out_specs=P("pair", "virt"),
        check_vma=False,
    )
```

```python
import functools

import jax
import jax.numpy as jnp
import numpy as np
from jax import lax
from jax.experimental import pallas as pl
from jax.experimental.pallas import tpu as pltpu
from jax.sharding import PartitionSpec as P

TILE = 128
AXES = ("pair", "virt")
N = 4
SENT = jnp.float16
FLIP = {0: 0, 1: -1, -1: 1, 2: 2}


def lin(z, y, x, c):
    return ((z % N) * N + y % N) * 2 * N + (x % N) * 2 + c


def permute(arr, to):
    pairs = [
        (lin(z, y, x, c), lin(*to(z, y, x, c)))
        for z in range(N)
        for y in range(N)
        for x in range(N)
        for c in range(2)
    ]
    return lax.ppermute(arr, AXES, pairs)


def side(c):
    return -1 if c == 0 else 1


def swap(arr):
    return permute(arr, lambda z, y, x, c: (z, y, x, 1 - c))


def shift(arr, axis):
    if axis == "x":
        return permute(arr, lambda z, y, x, c: (z, y, x - side(c), c))
    return permute(arr, lambda z, y, x, c: (z, y - side(c), x, c))


def swapped(item):
    (arr,), offs, koffs, flip = item
    return (swap(arr),), tuple(FLIP[o] for o in offs), tuple(FLIP[o] for o in koffs), not flip


def tie(value, *others):
    return lax.optimization_barrier((value, *others))[0]


def first_round(own, other, axis):
    near = shift(jnp.concatenate([own, other], 0), axis)
    far = shift(near[:1], axis)
    near_swapped, far_swapped = swap(near), swap(far)
    return {
        (0, 0): own,
        (0, 1): other,
        (1, 0): near[:1],
        (1, 1): near[1:],
        (-1, 1): near_swapped[:1],
        (-1, 0): near_swapped[1:],
        (2, 0): far,
        (2, 1): far_swapped,
    }


def screen_amps(mask_ref, amps_ref, *out_refs):
    starts = np.cumsum([0] + [o.shape[1] for o in out_refs]).tolist()
    for out_ref, lo, hi in zip(out_refs, starts, starts[1:]):
        cuts = [lo, *range((lo // TILE + 1) * TILE, hi, TILE), hi]
        for top, end in zip(cuts, cuts[1:]):
            top_tile = top // TILE
            for j in range(amps_ref.shape[1] // TILE):
                tile = amps_ref[top:end, j * TILE : (j + 1) * TILE]
                out_ref[0, top - lo : end - lo, j * TILE : (j + 1) * TILE] = jnp.where(
                    mask_ref[top_tile, j] != 0, tile, jnp.zeros_like(tile)
                )


def screen_ints(mask_ref, ints_ref, out_ref):
    step = pl.program_id(0)
    n = ints_ref.shape[0] // TILE
    for i in range(n):
        for j in range(ints_ref.shape[1] // TILE):
            tile = ints_ref[i * TILE : (i + 1) * TILE, j * TILE : (j + 1) * TILE]
            out_ref[i * TILE : (i + 1) * TILE, j * TILE : (j + 1) * TILE] = jnp.where(
                mask_ref[step * n + i, j] != 0, tile, jnp.zeros_like(tile)
            )


OFFS = (0, 1, -1, 2)
CORE = 4


def product_kernel(phases, n_init, n_out, table_ref, where_ref, *refs):
    n = sum(count for _, _, lanes in phases for count, _, _ in lanes)
    a_refs, kept_ref, init_refs, out_refs = refs[:n], refs[n], refs[n + 1 : n + 1 + n_init], refs[-n_out:]
    s = pl.program_id(0)
    core = where_ref[CORE]
    rows = out_refs[0].shape[0]

    def add(places, lanes):
        sides = []
        for first, second in lanes:
            sides.append(jnp.concatenate([first, second], -1))
        a = sides[0] if len(sides) == 1 else jnp.concatenate(sides, 0)
        part = jnp.dot(a, kept_ref[...], preferred_element_type=jnp.float32)
        for i, o in enumerate(places):
            mine = part[i * rows : (i + 1) * rows]

            @pl.when(s == 0)
            def _():
                out_refs[o][...] = mine + init_refs[o][...] if n_init else mine

            @pl.when(s != 0)
            def _():
                out_refs[o][...] += mine

    at = 0
    for lo, hi, lanes in phases:
        places, blocks, split = [], [], None
        for count, order, flip in lanes:
            places += order
            if count == 2:
                split = a_refs[at], a_refs[at + 1]
            elif flip is None:
                blocks.append((a_refs[at], 0))
            else:
                blocks.append((a_refs[at], 1 - core if flip else core))
            at += count

        if split is None:

            @pl.when((s >= lo) & (s < hi))
            def _():
                add(places, [(ref[0, i], ref[0, 1 - i]) for ref, i in blocks])
        else:
            for here in (0, 1):

                @pl.when((s >= lo) & (s < hi) & (core == here))
                def _():
                    other = split[1][0]
                    if len(places) > 1:
                        turned = [places.index(OFFS.index(FLIP[OFFS[o]])) for o in places]
                        other = jnp.concatenate([other[i * rows : (i + 1) * rows] for i in turned], 0)
                    pair = split[0][0], other
                    add(places, [pair if here == 0 else pair[::-1]])


def product(groups, offs, kept, where, init=()):
    phases, total = [], 0
    for group in groups:
        steps = len(group[0][2])
        phases.append((total, total + steps, [(len(arrs), [offs.index(o) for o in order], flip) for arrs, order, _, flip in group]))
        total += steps
    arrs, table = [], []
    where_row = np.zeros(total, np.int32)
    for group, (lo, hi, _) in zip(groups, phases):
        wanted = group[0][2]
        for item in group:
            for i, arr in enumerate(item[0]):
                stored = item[2] if i == 0 else tuple(FLIP[o] for o in item[2])
                places = [stored.index(o) for o in wanted]
                row = np.zeros(total, np.int32)
                row[:lo], row[lo:hi], row[hi:] = places[0], places, places[-1]
                arrs.append(arr)
                table.append(row)
        where_row[lo:hi] = [OFFS.index(o) for o in wanted]
    table = np.stack(table + [where_row])
    rows, depth = arrs[0].shape[-2] // len(groups[0][0][1]), arrs[0].shape[-1]
    width, nf = kept.shape[1], len(offs)
    a_specs = [
        pl.BlockSpec((1,) + arr.shape[1:], lambda s, t, w, i=i, nd=arr.ndim: (t[i, s],) + (0,) * (nd - 1))
        for i, arr in enumerate(arrs)
    ]
    flat = pl.BlockSpec((rows, width), lambda s, t, w: (0, 0))
    return pl.pallas_call(
        functools.partial(product_kernel, phases, len(init), nf),
        grid_spec=pltpu.PrefetchScalarGridSpec(
            num_scalar_prefetch=2,
            grid=(total,),
            in_specs=a_specs
            + [pl.BlockSpec((2 * depth, width), lambda s, t, w: (w[t[len(arrs), s]], 0))]
            + [flat] * len(init),
            out_specs=[flat] * nf,
        ),
        out_shape=[jax.ShapeDtypeStruct((rows, width), jnp.float32)] * nf,
        compiler_params=pltpu.CompilerParams(vmem_limit_bytes=VMEM_BYTES),
        cost_estimate=pl.CostEstimate(
            flops=rows * nf * depth * width * total // 4,
            bytes_accessed=total * depth * (nf * rows + width) // 4,
            transcendentals=0,
        ),
    )(jnp.asarray(table), where, *arrs, kept, *init)


VMEM_BYTES = 16 << 20


M_ROWS = 192


def product_plane_kernel(ys, planes_ref, kept_ref, *refs):
    out_refs, (a_buf, b_buf, a_sem, b_sem) = refs[: len(ys)], refs[len(ys) :]
    rows, depth = a_buf.shape[-2:]

    def copies(step):
        kept = pltpu.make_async_copy(kept_ref.at[pl.ds(step * 2 * depth, 2 * depth)], b_buf.at[step], b_sem.at[step])
        return [kept] + [
            pltpu.make_async_copy(planes_ref.at[y, pl.ds(2 * step, 2)], a_buf.at[step, i], a_sem.at[step, i])
            for i, y in enumerate(ys)
        ]

    for step in range(N):
        for copy in copies(step):
            copy.start()
    for step in range(N):
        for copy in copies(step):
            copy.wait()
        for i, out_ref in enumerate(out_refs):
            for m in range(0, rows, M_ROWS):
                here = slice(m, min(m + M_ROWS, rows))
                a = jnp.concatenate([a_buf[step, i, 0, here], a_buf[step, i, 1, here]], -1)
                part = jnp.dot(a, b_buf[step], preferred_element_type=jnp.float32)
                out_ref[here] = part if step == 0 else out_ref[here] + part


def product_plane(planes, ys, kept):
    _, _, rows, depth = planes.shape
    width = kept.shape[1]
    return pl.pallas_call(
        functools.partial(product_plane_kernel, ys),
        in_specs=[pl.BlockSpec(memory_space=pltpu.HBM)] * 2,
        out_specs=[pl.BlockSpec(memory_space=pltpu.VMEM)] * len(ys),
        out_shape=[jax.ShapeDtypeStruct((rows, width), jnp.float32)] * len(ys),
        scratch_shapes=[
            pltpu.VMEM((N, len(ys), 2, rows, depth), planes.dtype),
            pltpu.VMEM((N, 2 * depth, width), kept.dtype),
            pltpu.SemaphoreType.DMA((N, len(ys))),
            pltpu.SemaphoreType.DMA((N,)),
        ],
        compiler_params=pltpu.CompilerParams(vmem_limit_bytes=30 << 20),
        cost_estimate=pl.CostEstimate(
            flops=4 * N * len(ys) * rows * depth * width,
            bytes_accessed=4 * N * depth * (len(ys) * rows + width) + 4 * len(ys) * rows * width,
            transcendentals=0,
        ),
    )(planes, kept)


def to_owner(part, off):
    step = lambda c: off * side(c) if abs(off) == 1 else off
    return permute(part.astype(SENT), lambda z, y, x, c: (z + y + step(c), y, x, c))


S_ROWS, A_ROWS, B_ROWS = 368, 64, 80


def on_device(amps, ints, amp_mask, int_mask, vir_energy, pair_energy):
    rows, depth = amps.shape
    split = (S_ROWS, A_ROWS, B_ROWS)
    screened = pl.pallas_call(
        screen_amps,
        in_specs=[pl.BlockSpec(memory_space=pltpu.SMEM), pl.BlockSpec(memory_space=pltpu.VMEM)],
        out_specs=[pl.BlockSpec(memory_space=pltpu.VMEM)] * len(split),
        out_shape=[jax.ShapeDtypeStruct((1, r, depth), amps.dtype) for r in split],
    )(amp_mask, amps)
    s_part, a_part, b_part = [permute(part, lambda z, y, x, c: (y, z - y, x, c)) for part in screened]
    width = ints.shape[1]
    kept = pl.pallas_call(
        screen_ints,
        grid_spec=pltpu.PrefetchScalarGridSpec(
            num_scalar_prefetch=1,
            grid=(ints.shape[0] // depth,),
            in_specs=[pl.BlockSpec((depth, width), lambda s, m: (s, 0))],
            out_specs=pl.BlockSpec((depth, width), lambda s, m: (s, 0)),
        ),
        out_shape=jax.ShapeDtypeStruct(ints.shape, ints.dtype),
        compiler_params=pltpu.CompilerParams(vmem_limit_bytes=VMEM_BYTES),
    )(int_mask, ints)
    virt = lax.axis_index("virt")
    core, x = virt % 2, (virt // 2) % N
    d = 2 * core - 1
    where = jnp.stack([(x + o * (d if abs(o) == 1 else 1)) % N for o in OFFS] + [core]).astype(jnp.int32)

    a_part, b_part, kept = lax.optimization_barrier((a_part, b_part, kept))
    a_pair, b_pair = swap(a_part), swap(b_part)
    s_part = lax.optimization_barrier((s_part, kept))[0]
    planes = lax.all_gather(s_part[0], "virt", axis=0).reshape(N, 2 * N, S_ROWS, depth)
    round_a, round_b = first_round(a_part, a_pair, "x"), first_round(b_part, b_pair, "y")
    a_own = ((jnp.concatenate([round_a[o, k] for o in OFFS for k in (0, 1)], 0).reshape(N, 2, A_ROWS, depth),), (0,), OFFS, False)
    b_own = (
        (jnp.concatenate([round_b[o, k] for k in (0, 1) for o in OFFS], 0).reshape(1, 2, N * B_ROWS, depth),),
        OFFS,
        (0,),
        False,
    )
    a_near, b_near = ((shift(a_own[0][0], "y"),), (1,), OFFS, False), ((shift(b_own[0][0], "x"),), OFFS, (1,), False)
    a_next, b_next = a_near[0][0][:, 0], b_near[0][0][:, 0]
    a_far, b_far = shift(a_next, "y"), shift(b_next, "x")
    a_side, b_side = swapped(a_near), swapped(b_near)

    b_early = product([[b_own], [b_near], [b_side]], OFFS, kept, where)
    a_early = product([[a_own, a_near, a_side]], OFFS[:3], kept, where)
    a_far, b_far = lax.optimization_barrier((a_far, b_far, b_early, a_early))[:2]
    a_other, b_other = swap(a_far), swap(b_far)
    b_done = product([[((b_far, b_other), OFFS, (2,), False)]], OFFS, kept, where, b_early)
    a_last = product([[((a_far, a_other), (2,), OFFS, False)]], (2,), kept, where)
    p_parts = [jnp.concatenate([a, b], 0).astype(SENT) for a, b in zip([*a_early, *a_last], b_done)]
    p_got = [to_owner(part, o) for part, o in zip(p_parts, OFFS)]
    planes = lax.optimization_barrier((planes, p_parts))[0]
    turn = lambda part, i: permute(part.astype(SENT), lambda z, y, x, c: (z + i, y, x, c))
    (across,) = product_plane(planes, (2,), kept)
    across = permute(across.astype(SENT), lambda z, y, x, c: (z - side(c), y, x, c)).astype(jnp.float32)
    up, down = product_plane(planes, (1, 3), kept)
    up = (up + jnp.where(core == 0, across, 0.0)).astype(SENT)
    down = (down + jnp.where(core == 1, across, 0.0)).astype(SENT)
    planes, up, down = lax.optimization_barrier((planes, up, down))
    up, down = turn(up, 1), turn(down, 3)
    (here,) = product_plane(planes, (0,), kept)
    s_got = [here, up, down]

    total = lambda got: sum(g.astype(jnp.float32) for g in got)
    contracted = jnp.concatenate([total(s_got), total(p_got)], 0)
    denom = vir_energy[None, :] - pair_energy[:, None]
    return amps.astype(jnp.float32) + contracted / denom


def solution(mesh):
    return jax.shard_map(
        on_device,
        mesh=mesh,
        in_specs=(
            P("pair", "virt"),
            P("pair", "virt"),
            P("pair", "virt"),
            P("pair", "virt"),
            P("virt"),
            P("pair"),
        ),
        out_specs=P("pair", "virt"),
        check_vma=False,
    )
```

```python
import functools

import jax
import jax.numpy as jnp
import numpy as np
from jax import lax
from jax.experimental import pallas as pl
from jax.experimental.pallas import tpu as pltpu
from jax.sharding import PartitionSpec as P

TILE = 128
AXES = ("pair", "virt")
N = 4
SENT = jnp.float16
GAIN = 8.0
FLIP = {0: 0, 1: -1, -1: 1, 2: 2}


def lin(z, y, x, c):
    return ((z % N) * N + y % N) * 2 * N + (x % N) * 2 + c


def permute(arr, to):
    pairs = [
        (lin(z, y, x, c), lin(*to(z, y, x, c)))
        for z in range(N)
        for y in range(N)
        for x in range(N)
        for c in range(2)
    ]
    return lax.ppermute(arr, AXES, pairs)


def side(c):
    return -1 if c == 0 else 1


def swap(arr):
    return permute(arr, lambda z, y, x, c: (z, y, x, 1 - c))


def shift(arr, axis):
    if axis == "x":
        return permute(arr, lambda z, y, x, c: (z, y, x - side(c), c))
    return permute(arr, lambda z, y, x, c: (z, y - side(c), x, c))


def swapped(item):
    (arr,), offs, koffs, flip = item
    return (swap(arr),), tuple(FLIP[o] for o in offs), tuple(FLIP[o] for o in koffs), not flip


def tie(value, *others):
    return lax.optimization_barrier((value, *others))[0]


def first_round(own, other, axis):
    near = shift(jnp.concatenate([own, other], 0), axis)
    far = shift(near[:1], axis)
    near_swapped, far_swapped = swap(near), swap(far)
    return {
        (0, 0): own,
        (0, 1): other,
        (1, 0): near[:1],
        (1, 1): near[1:],
        (-1, 1): near_swapped[:1],
        (-1, 0): near_swapped[1:],
        (2, 0): far,
        (2, 1): far_swapped,
    }


def screen_amps(mask_ref, amps_ref, *out_refs):
    starts = np.cumsum([0] + [o.shape[1] for o in out_refs]).tolist()
    for out_ref, lo, hi in zip(out_refs, starts, starts[1:]):
        cuts = [lo, *range((lo // TILE + 1) * TILE, hi, TILE), hi]
        for top, end in zip(cuts, cuts[1:]):
            top_tile = top // TILE
            for j in range(amps_ref.shape[1] // TILE):
                tile = amps_ref[top:end, j * TILE : (j + 1) * TILE]
                out_ref[0, top - lo : end - lo, j * TILE : (j + 1) * TILE] = jnp.where(
                    mask_ref[top_tile, j] != 0, tile, jnp.zeros_like(tile)
                )


def screen_ints(mask_ref, ints_ref, out_ref):
    step = pl.program_id(0)
    n = ints_ref.shape[0] // TILE
    for i in range(n):
        for j in range(ints_ref.shape[1] // TILE):
            tile = ints_ref[i * TILE : (i + 1) * TILE, j * TILE : (j + 1) * TILE]
            out_ref[i * TILE : (i + 1) * TILE, j * TILE : (j + 1) * TILE] = jnp.where(
                mask_ref[step * n + i, j] != 0, tile, jnp.zeros_like(tile)
            )


OFFS = (0, 1, -1, 2)
CORE = 4


def product_kernel(phases, n_init, n_out, table_ref, where_ref, *refs):
    n = sum(count for _, _, lanes in phases for count, _, _ in lanes)
    a_refs, kept_ref, init_refs, out_refs = refs[:n], refs[n], refs[n + 1 : n + 1 + n_init], refs[-n_out:]
    s = pl.program_id(0)
    core = where_ref[CORE]
    rows = out_refs[0].shape[0]

    def add(places, lanes):
        sides = []
        for first, second in lanes:
            sides.append(jnp.concatenate([first, second], -1))
        a = sides[0] if len(sides) == 1 else jnp.concatenate(sides, 0)
        part = jnp.dot(a, kept_ref[...], preferred_element_type=jnp.float32)
        for i, o in enumerate(places):
            mine = part[i * rows : (i + 1) * rows]

            @pl.when(s == 0)
            def _():
                out_refs[o][...] = mine + init_refs[o][...] if n_init else mine

            @pl.when(s != 0)
            def _():
                out_refs[o][...] += mine

    at = 0
    for lo, hi, lanes in phases:
        places, blocks, split = [], [], None
        for count, order, flip in lanes:
            places += order
            if count == 2:
                split = a_refs[at], a_refs[at + 1]
            elif flip is None:
                blocks.append((a_refs[at], 0))
            else:
                blocks.append((a_refs[at], 1 - core if flip else core))
            at += count

        if split is None:

            @pl.when((s >= lo) & (s < hi))
            def _():
                add(places, [(ref[0, i], ref[0, 1 - i]) for ref, i in blocks])
        else:
            for here in (0, 1):

                @pl.when((s >= lo) & (s < hi) & (core == here))
                def _():
                    other = split[1][0]
                    if len(places) > 1:
                        turned = [places.index(OFFS.index(FLIP[OFFS[o]])) for o in places]
                        other = jnp.concatenate([other[i * rows : (i + 1) * rows] for i in turned], 0)
                    pair = split[0][0], other
                    add(places, [pair if here == 0 else pair[::-1]])


def product(groups, offs, kept, where, init=()):
    phases, total = [], 0
    for group in groups:
        steps = len(group[0][2])
        phases.append((total, total + steps, [(len(arrs), [offs.index(o) for o in order], flip) for arrs, order, _, flip in group]))
        total += steps
    arrs, table = [], []
    where_row = np.zeros(total, np.int32)
    for group, (lo, hi, _) in zip(groups, phases):
        wanted = group[0][2]
        for item in group:
            for i, arr in enumerate(item[0]):
                stored = item[2] if i == 0 else tuple(FLIP[o] for o in item[2])
                places = [stored.index(o) for o in wanted]
                row = np.zeros(total, np.int32)
                row[:lo], row[lo:hi], row[hi:] = places[0], places, places[-1]
                arrs.append(arr)
                table.append(row)
        where_row[lo:hi] = [OFFS.index(o) for o in wanted]
    table = np.stack(table + [where_row])
    rows, depth = arrs[0].shape[-2] // len(groups[0][0][1]), arrs[0].shape[-1]
    width, nf = kept.shape[1], len(offs)
    a_specs = [
        pl.BlockSpec((1,) + arr.shape[1:], lambda s, t, w, i=i, nd=arr.ndim: (t[i, s],) + (0,) * (nd - 1))
        for i, arr in enumerate(arrs)
    ]
    flat = pl.BlockSpec((rows, width), lambda s, t, w: (0, 0))
    return pl.pallas_call(
        functools.partial(product_kernel, phases, len(init), nf),
        grid_spec=pltpu.PrefetchScalarGridSpec(
            num_scalar_prefetch=2,
            grid=(total,),
            in_specs=a_specs
            + [pl.BlockSpec((2 * depth, width), lambda s, t, w: (w[t[len(arrs), s]], 0))]
            + [flat] * len(init),
            out_specs=[flat] * nf,
        ),
        out_shape=[jax.ShapeDtypeStruct((rows, width), jnp.float32)] * nf,
        compiler_params=pltpu.CompilerParams(vmem_limit_bytes=VMEM_BYTES),
        cost_estimate=pl.CostEstimate(
            flops=rows * nf * depth * width * total // 4,
            bytes_accessed=total * depth * (nf * rows + width) // 4,
            transcendentals=0,
        ),
    )(jnp.asarray(table), where, *arrs, kept, *init)


VMEM_BYTES = 16 << 20


M_ROWS = 192


def product_plane_kernel(ys, planes_ref, kept_ref, *refs):
    out_refs, (a_buf, b_buf, a_sem, b_sem) = refs[: len(ys)], refs[len(ys) :]
    rows, depth = a_buf.shape[-2:]

    def copies(step):
        kept = pltpu.make_async_copy(kept_ref.at[pl.ds(step * 2 * depth, 2 * depth)], b_buf.at[step], b_sem.at[step])
        return [kept] + [
            pltpu.make_async_copy(planes_ref.at[y, pl.ds(2 * step, 2)], a_buf.at[step, i], a_sem.at[step, i])
            for i, y in enumerate(ys)
        ]

    for step in range(N):
        for copy in copies(step):
            copy.start()
    for step in range(N):
        for copy in copies(step):
            copy.wait()
        for i, out_ref in enumerate(out_refs):
            for m in range(0, rows, M_ROWS):
                here = slice(m, min(m + M_ROWS, rows))
                a = jnp.concatenate([a_buf[step, i, 0, here], a_buf[step, i, 1, here]], -1)
                part = jnp.dot(a, b_buf[step], preferred_element_type=jnp.float32)
                out_ref[here] = part if step == 0 else out_ref[here] + part


def product_plane(planes, ys, kept):
    _, _, rows, depth = planes.shape
    width = kept.shape[1]
    return pl.pallas_call(
        functools.partial(product_plane_kernel, ys),
        in_specs=[pl.BlockSpec(memory_space=pltpu.HBM)] * 2,
        out_specs=[pl.BlockSpec(memory_space=pltpu.VMEM)] * len(ys),
        out_shape=[jax.ShapeDtypeStruct((rows, width), jnp.float32)] * len(ys),
        scratch_shapes=[
            pltpu.VMEM((N, len(ys), 2, rows, depth), planes.dtype),
            pltpu.VMEM((N, 2 * depth, width), kept.dtype),
            pltpu.SemaphoreType.DMA((N, len(ys))),
            pltpu.SemaphoreType.DMA((N,)),
        ],
        compiler_params=pltpu.CompilerParams(vmem_limit_bytes=30 << 20),
        cost_estimate=pl.CostEstimate(
            flops=4 * N * len(ys) * rows * depth * width,
            bytes_accessed=4 * N * depth * (len(ys) * rows + width) + 4 * len(ys) * rows * width,
            transcendentals=0,
        ),
    )(planes, kept)


def to_owner(part, off):
    step = lambda c: off * side(c) if abs(off) == 1 else off
    return permute(part, lambda z, y, x, c: (z + y + step(c), y, x, c))


S_ROWS, A_ROWS, B_ROWS = 368, 64, 80


def on_device(amps, ints, amp_mask, int_mask, vir_energy, pair_energy):
    rows, depth = amps.shape
    split = (S_ROWS, A_ROWS, B_ROWS)
    screened = pl.pallas_call(
        screen_amps,
        in_specs=[pl.BlockSpec(memory_space=pltpu.SMEM), pl.BlockSpec(memory_space=pltpu.VMEM)],
        out_specs=[pl.BlockSpec(memory_space=pltpu.VMEM)] * len(split),
        out_shape=[jax.ShapeDtypeStruct((1, r, depth), amps.dtype) for r in split],
    )(amp_mask, amps)
    s_part, a_part, b_part = [permute(part, lambda z, y, x, c: (y, z - y, x, c)) for part in screened]
    width = ints.shape[1]
    kept = pl.pallas_call(
        screen_ints,
        grid_spec=pltpu.PrefetchScalarGridSpec(
            num_scalar_prefetch=1,
            grid=(ints.shape[0] // depth,),
            in_specs=[pl.BlockSpec((depth, width), lambda s, m: (s, 0))],
            out_specs=pl.BlockSpec((depth, width), lambda s, m: (s, 0)),
        ),
        out_shape=jax.ShapeDtypeStruct(ints.shape, ints.dtype),
        compiler_params=pltpu.CompilerParams(vmem_limit_bytes=VMEM_BYTES),
    )(int_mask, ints)
    virt = lax.axis_index("virt")
    core, x = virt % 2, (virt // 2) % N
    d = 2 * core - 1
    where = jnp.stack([(x + o * (d if abs(o) == 1 else 1)) % N for o in OFFS] + [core]).astype(jnp.int32)

    a_part, b_part, kept = lax.optimization_barrier((a_part, b_part, kept))
    a_pair, b_pair = swap(a_part), swap(b_part)
    s_part = lax.optimization_barrier((s_part, kept))[0]
    planes = lax.all_gather(s_part[0], "virt", axis=0).reshape(N, 2 * N, S_ROWS, depth)
    round_a, round_b = first_round(a_part, a_pair, "x"), first_round(b_part, b_pair, "y")
    a_own = ((jnp.concatenate([round_a[o, k] for o in OFFS for k in (0, 1)], 0).reshape(N, 2, A_ROWS, depth),), (0,), OFFS, False)
    b_own = (
        (jnp.concatenate([round_b[o, k] for k in (0, 1) for o in OFFS], 0).reshape(1, 2, N * B_ROWS, depth),),
        OFFS,
        (0,),
        False,
    )
    a_near, b_near = ((shift(a_own[0][0], "y"),), (1,), OFFS, False), ((shift(b_own[0][0], "x"),), OFFS, (1,), False)
    a_next, b_next = a_near[0][0][:, 0], b_near[0][0][:, 0]
    a_far, b_far = shift(a_next, "y"), shift(b_next, "x")
    a_side, b_side = swapped(a_near), swapped(b_near)

    b_early = product([[b_own], [b_near], [b_side]], OFFS, kept, where)
    a_early = product([[a_own, a_near, a_side]], OFFS[:3], kept, where)
    a_far, b_far = lax.optimization_barrier((a_far, b_far, b_early, a_early))[:2]
    a_other, b_other = swap(a_far), swap(b_far)
    b_done = product([[((b_far, b_other), OFFS, (2,), False)]], OFFS, kept, where, b_early)
    a_last = product([[((a_far, a_other), (2,), OFFS, False)]], (2,), kept, where)
    p_parts = [(jnp.concatenate([a, b], 0) * GAIN).astype(SENT) for a, b in zip([*a_early, *a_last], b_done)]
    p_got = [to_owner(part, o) for part, o in zip(p_parts, OFFS)]
    planes = lax.optimization_barrier((planes, p_parts))[0]
    turn = lambda part, i: permute(part, lambda z, y, x, c: (z + i, y, x, c))
    (across,) = product_plane(planes, (2,), kept)
    across = permute((across * GAIN).astype(SENT), lambda z, y, x, c: (z - side(c), y, x, c)).astype(jnp.float32)
    up, down = product_plane(planes, (1, 3), kept)
    up = (up * GAIN + jnp.where(core == 0, across, 0.0)).astype(SENT)
    down = (down * GAIN + jnp.where(core == 1, across, 0.0)).astype(SENT)
    planes, up, down = lax.optimization_barrier((planes, up, down))
    up, down = turn(up, 1), turn(down, 3)
    (here,) = product_plane(planes, (0,), kept)
    s_got = [here * GAIN, up, down]

    total = lambda got: sum(g.astype(jnp.float32) for g in got)
    contracted = jnp.concatenate([total(s_got), total(p_got)], 0)
    denom = vir_energy[None, :] - pair_energy[:, None]
    return amps.astype(jnp.float32) + contracted / (GAIN * denom)


def solution(mesh):
    return jax.shard_map(
        on_device,
        mesh=mesh,
        in_specs=(
            P("pair", "virt"),
            P("pair", "virt"),
            P("pair", "virt"),
            P("pair", "virt"),
            P("virt"),
            P("pair"),
        ),
        out_specs=P("pair", "virt"),
        check_vma=False,
    )
```

```python
import functools

import jax
import jax.numpy as jnp
import numpy as np
from jax import lax
from jax.experimental import pallas as pl
from jax.experimental.pallas import tpu as pltpu
from jax.sharding import PartitionSpec as P

TILE = 128
AXES = ("pair", "virt")
N = 4
SENT = jnp.float16
GAIN = 8.0
FLIP = {0: 0, 1: -1, -1: 1, 2: 2}


def lin(z, y, x, c):
    return ((z % N) * N + y % N) * 2 * N + (x % N) * 2 + c


def permute(arr, to):
    pairs = [
        (lin(z, y, x, c), lin(*to(z, y, x, c)))
        for z in range(N)
        for y in range(N)
        for x in range(N)
        for c in range(2)
    ]
    return lax.ppermute(arr, AXES, pairs)


def side(c):
    return -1 if c == 0 else 1


def swap(arr):
    return permute(arr, lambda z, y, x, c: (z, y, x, 1 - c))


def shift(arr, axis):
    if axis == "x":
        return permute(arr, lambda z, y, x, c: (z, y, x - side(c), c))
    return permute(arr, lambda z, y, x, c: (z, y - side(c), x, c))


def swapped(item):
    (arr,), offs, koffs, flip = item
    return (swap(arr),), tuple(FLIP[o] for o in offs), tuple(FLIP[o] for o in koffs), not flip


def tie(value, *others):
    return lax.optimization_barrier((value, *others))[0]


def first_round(own, other, axis):
    near = shift(jnp.concatenate([own, other], 0), axis)
    far = shift(near[:1], axis)
    near_swapped, far_swapped = swap(near), swap(far)
    return {
        (0, 0): own,
        (0, 1): other,
        (1, 0): near[:1],
        (1, 1): near[1:],
        (-1, 1): near_swapped[:1],
        (-1, 0): near_swapped[1:],
        (2, 0): far,
        (2, 1): far_swapped,
    }


def screen_amps(mask_ref, amps_ref, *out_refs):
    starts = np.cumsum([0] + [o.shape[1] for o in out_refs]).tolist()
    for out_ref, lo, hi in zip(out_refs, starts, starts[1:]):
        cuts = [lo, *range((lo // TILE + 1) * TILE, hi, TILE), hi]
        for top, end in zip(cuts, cuts[1:]):
            top_tile = top // TILE
            for j in range(amps_ref.shape[1] // TILE):
                tile = amps_ref[top:end, j * TILE : (j + 1) * TILE]
                out_ref[0, top - lo : end - lo, j * TILE : (j + 1) * TILE] = jnp.where(
                    mask_ref[top_tile, j] != 0, tile, jnp.zeros_like(tile)
                )


def screen_ints(mask_ref, ints_ref, out_ref):
    step = pl.program_id(0)
    n = ints_ref.shape[0] // TILE
    for i in range(n):
        for j in range(ints_ref.shape[1] // TILE):
            tile = ints_ref[i * TILE : (i + 1) * TILE, j * TILE : (j + 1) * TILE]
            out_ref[i * TILE : (i + 1) * TILE, j * TILE : (j + 1) * TILE] = jnp.where(
                mask_ref[step * n + i, j] != 0, tile, jnp.zeros_like(tile)
            )


OFFS = (0, 1, -1, 2)
CORE = 4


def product_kernel(phases, n_init, n_out, table_ref, where_ref, *refs):
    n = sum(count for _, _, lanes in phases for count, _, _ in lanes)
    a_refs, kept_ref, init_refs, out_refs = refs[:n], refs[n], refs[n + 1 : n + 1 + n_init], refs[-n_out:]
    s = pl.program_id(0)
    core = where_ref[CORE]
    rows = out_refs[0].shape[0]

    def add(places, lanes):
        sides = []
        for first, second in lanes:
            sides.append(jnp.concatenate([first, second], -1))
        a = sides[0] if len(sides) == 1 else jnp.concatenate(sides, 0)
        part = jnp.dot(a, kept_ref[...], preferred_element_type=jnp.float32)
        for i, o in enumerate(places):
            mine = part[i * rows : (i + 1) * rows]

            @pl.when(s == 0)
            def _():
                out_refs[o][...] = mine + init_refs[o][...] if n_init else mine

            @pl.when(s != 0)
            def _():
                out_refs[o][...] += mine

    at = 0
    for lo, hi, lanes in phases:
        places, blocks, split = [], [], None
        for count, order, flip in lanes:
            places += order
            if count == 2:
                split = a_refs[at], a_refs[at + 1]
            elif flip is None:
                blocks.append((a_refs[at], 0))
            else:
                blocks.append((a_refs[at], 1 - core if flip else core))
            at += count

        if split is None:

            @pl.when((s >= lo) & (s < hi))
            def _():
                add(places, [(ref[0, i], ref[0, 1 - i]) for ref, i in blocks])
        else:
            for here in (0, 1):

                @pl.when((s >= lo) & (s < hi) & (core == here))
                def _():
                    other = split[1][0]
                    if len(places) > 1:
                        turned = [places.index(OFFS.index(FLIP[OFFS[o]])) for o in places]
                        other = jnp.concatenate([other[i * rows : (i + 1) * rows] for i in turned], 0)
                    pair = split[0][0], other
                    add(places, [pair if here == 0 else pair[::-1]])


def product(groups, offs, kept, where, init=()):
    phases, total = [], 0
    for group in groups:
        steps = len(group[0][2])
        phases.append((total, total + steps, [(len(arrs), [offs.index(o) for o in order], flip) for arrs, order, _, flip in group]))
        total += steps
    arrs, table = [], []
    where_row = np.zeros(total, np.int32)
    for group, (lo, hi, _) in zip(groups, phases):
        wanted = group[0][2]
        for item in group:
            for i, arr in enumerate(item[0]):
                stored = item[2] if i == 0 else tuple(FLIP[o] for o in item[2])
                places = [stored.index(o) for o in wanted]
                row = np.zeros(total, np.int32)
                row[:lo], row[lo:hi], row[hi:] = places[0], places, places[-1]
                arrs.append(arr)
                table.append(row)
        where_row[lo:hi] = [OFFS.index(o) for o in wanted]
    table = np.stack(table + [where_row])
    rows, depth = arrs[0].shape[-2] // len(groups[0][0][1]), arrs[0].shape[-1]
    width, nf = kept.shape[1], len(offs)
    a_specs = [
        pl.BlockSpec((1,) + arr.shape[1:], lambda s, t, w, i=i, nd=arr.ndim: (t[i, s],) + (0,) * (nd - 1))
        for i, arr in enumerate(arrs)
    ]
    flat = pl.BlockSpec((rows, width), lambda s, t, w: (0, 0))
    return pl.pallas_call(
        functools.partial(product_kernel, phases, len(init), nf),
        grid_spec=pltpu.PrefetchScalarGridSpec(
            num_scalar_prefetch=2,
            grid=(total,),
            in_specs=a_specs
            + [pl.BlockSpec((2 * depth, width), lambda s, t, w: (w[t[len(arrs), s]], 0))]
            + [flat] * len(init),
            out_specs=[flat] * nf,
        ),
        out_shape=[jax.ShapeDtypeStruct((rows, width), jnp.float32)] * nf,
        compiler_params=pltpu.CompilerParams(vmem_limit_bytes=VMEM_BYTES),
        cost_estimate=pl.CostEstimate(
            flops=rows * nf * depth * width * total // 4,
            bytes_accessed=total * depth * (nf * rows + width) // 4,
            transcendentals=0,
        ),
    )(jnp.asarray(table), where, *arrs, kept, *init)


VMEM_BYTES = 16 << 20


M_ROWS = 192


def product_plane_kernel(ys, planes_ref, kept_ref, *refs):
    out_refs, (a_buf, b_buf, a_sem, b_sem) = refs[: len(ys)], refs[len(ys) :]
    rows, depth = a_buf.shape[-2:]

    def copies(step):
        kept = pltpu.make_async_copy(kept_ref.at[pl.ds(step * 2 * depth, 2 * depth)], b_buf.at[step], b_sem.at[step])
        return [kept] + [
            pltpu.make_async_copy(planes_ref.at[y, pl.ds(2 * step, 2)], a_buf.at[step, i], a_sem.at[step, i])
            for i, y in enumerate(ys)
        ]

    for step in range(N):
        for copy in copies(step):
            copy.start()
    for step in range(N):
        for copy in copies(step):
            copy.wait()
        for i, out_ref in enumerate(out_refs):
            for m in range(0, rows, M_ROWS):
                here = slice(m, min(m + M_ROWS, rows))
                a = jnp.concatenate([a_buf[step, i, 0, here], a_buf[step, i, 1, here]], -1)
                part = jnp.dot(a, b_buf[step], preferred_element_type=jnp.float32)
                out_ref[here] = part if step == 0 else out_ref[here] + part


def product_plane(planes, ys, kept):
    _, _, rows, depth = planes.shape
    width = kept.shape[1]
    return pl.pallas_call(
        functools.partial(product_plane_kernel, ys),
        in_specs=[pl.BlockSpec(memory_space=pltpu.HBM)] * 2,
        out_specs=[pl.BlockSpec(memory_space=pltpu.VMEM)] * len(ys),
        out_shape=[jax.ShapeDtypeStruct((rows, width), jnp.float32)] * len(ys),
        scratch_shapes=[
            pltpu.VMEM((N, len(ys), 2, rows, depth), planes.dtype),
            pltpu.VMEM((N, 2 * depth, width), kept.dtype),
            pltpu.SemaphoreType.DMA((N, len(ys))),
            pltpu.SemaphoreType.DMA((N,)),
        ],
        compiler_params=pltpu.CompilerParams(vmem_limit_bytes=30 << 20),
        cost_estimate=pl.CostEstimate(
            flops=4 * N * len(ys) * rows * depth * width,
            bytes_accessed=4 * N * depth * (len(ys) * rows + width) + 4 * len(ys) * rows * width,
            transcendentals=0,
        ),
    )(planes, kept)


def to_owner(part, off):
    step = lambda c: off * side(c) if abs(off) == 1 else off
    return permute(part, lambda z, y, x, c: (z + y + step(c), y, x, c))


S_ROWS, A_ROWS, B_ROWS = 368, 64, 80


def on_device(amps, ints, amp_mask, int_mask, vir_energy, pair_energy):
    rows, depth = amps.shape
    split = (S_ROWS, A_ROWS, B_ROWS)
    screened = pl.pallas_call(
        screen_amps,
        in_specs=[pl.BlockSpec(memory_space=pltpu.SMEM), pl.BlockSpec(memory_space=pltpu.VMEM)],
        out_specs=[pl.BlockSpec(memory_space=pltpu.VMEM)] * len(split),
        out_shape=[jax.ShapeDtypeStruct((1, r, depth), amps.dtype) for r in split],
    )(amp_mask, amps)
    s_part, a_part, b_part = [permute(part, lambda z, y, x, c: (y, z - y, x, c)) for part in screened]
    width = ints.shape[1]
    kept = pl.pallas_call(
        screen_ints,
        grid_spec=pltpu.PrefetchScalarGridSpec(
            num_scalar_prefetch=1,
            grid=(ints.shape[0] // depth,),
            in_specs=[pl.BlockSpec((depth, width), lambda s, m: (s, 0))],
            out_specs=pl.BlockSpec((depth, width), lambda s, m: (s, 0)),
        ),
        out_shape=jax.ShapeDtypeStruct(ints.shape, ints.dtype),
        compiler_params=pltpu.CompilerParams(vmem_limit_bytes=VMEM_BYTES),
    )(int_mask, ints)
    virt = lax.axis_index("virt")
    core, x = virt % 2, (virt // 2) % N
    d = 2 * core - 1
    where = jnp.stack([(x + o * (d if abs(o) == 1 else 1)) % N for o in OFFS] + [core]).astype(jnp.int32)

    a_part, b_part, kept = lax.optimization_barrier((a_part, b_part, kept))
    a_pair, b_pair = swap(a_part), swap(b_part)
    s_part = lax.optimization_barrier((s_part, kept))[0]
    planes = lax.all_gather(s_part[0], "virt", axis=0).reshape(N, 2 * N, S_ROWS, depth)
    round_a, round_b = first_round(a_part, a_pair, "x"), first_round(b_part, b_pair, "y")
    a_own = ((jnp.concatenate([round_a[o, k] for o in OFFS for k in (0, 1)], 0).reshape(N, 2, A_ROWS, depth),), (0,), OFFS, False)
    b_own = (
        (jnp.concatenate([round_b[o, k] for k in (0, 1) for o in OFFS], 0).reshape(1, 2, N * B_ROWS, depth),),
        OFFS,
        (0,),
        False,
    )
    a_near, b_near = ((shift(a_own[0][0], "y"),), (1,), OFFS, False), ((shift(b_own[0][0], "x"),), OFFS, (1,), False)
    a_next, b_next = a_near[0][0][:, 0], b_near[0][0][:, 0]
    a_far, b_far = shift(a_next, "y"), shift(b_next, "x")
    a_side, b_side = swapped(a_near), swapped(b_near)

    b_early = product([[b_own], [b_near], [b_side]], OFFS, kept, where)
    a_early = product([[a_own, a_near, a_side]], OFFS[:3], kept, where)
    a_far, b_far = lax.optimization_barrier((a_far, b_far, b_early, a_early))[:2]
    a_other, b_other = swap(a_far), swap(b_far)
    b_done = product([[((b_far, b_other), OFFS, (2,), False)]], OFFS, kept, where, b_early)
    a_last = product([[((a_far, a_other), (2,), OFFS, False)]], (2,), kept, where)
    p_parts = [(jnp.concatenate([a, b], 0) * GAIN).astype(SENT) for a, b in zip([*a_early, *a_last], b_done)]
    p_got = [to_owner(part, o) for part, o in zip(p_parts, OFFS)]
    turn = lambda part, i: permute(part, lambda z, y, x, c: (z + i, y, x, c))
    (across,) = product_plane(planes, (2,), kept)
    across = permute((across * GAIN).astype(SENT), lambda z, y, x, c: (z - side(c), y, x, c)).astype(jnp.float32)
    up, down = product_plane(planes, (1, 3), kept)
    up = (up * GAIN + jnp.where(core == 0, across, 0.0)).astype(SENT)
    down = (down * GAIN + jnp.where(core == 1, across, 0.0)).astype(SENT)
    planes, up, down = lax.optimization_barrier((planes, up, down))
    up, down = turn(up, 1), turn(down, 3)
    (here,) = product_plane(planes, (0,), kept)
    s_got = [here * GAIN, up, down]

    total = lambda got: sum(g.astype(jnp.float32) for g in got)
    contracted = jnp.concatenate([total(s_got), total(p_got)], 0)
    denom = vir_energy[None, :] - pair_energy[:, None]
    return amps.astype(jnp.float32) + contracted / (GAIN * denom)


def solution(mesh):
    return jax.shard_map(
        on_device,
        mesh=mesh,
        in_specs=(
            P("pair", "virt"),
            P("pair", "virt"),
            P("pair", "virt"),
            P("pair", "virt"),
            P("virt"),
            P("pair"),
        ),
        out_specs=P("pair", "virt"),
        check_vma=False,
    )
```
